32 devices in a mesh: energy: 8 (over z, y), momentum: 4 (over x, core).
Axes of the slice: x: 2, y: 2, z: 4, core: 2. Of those that a mesh axis runs over, the one named last changes fastest.
Arguments:
- lesser: bfloat16 [8, 4, 2, 512, 512], P('energy', 'momentum'), may hold values from -6 to 6
- greater: bfloat16 [8, 4, 2, 512, 512], P('energy', 'momentum'), may hold values from -6 to 6
- retarded: bfloat16 [8, 4, 2, 512, 512], P('energy', 'momentum'), may hold values from -4.1875 to 4.1875
- occupation: float32 [2], replicated, may hold values from 0.1 to 2
- shift_slots: int32 [2, 2, 8], replicated, may hold values from 0 to 8, as said below
- coupling: int32 [2, 4, 4], replicated, may hold values from 1 to 8
Outputs:
- lesser_new: bfloat16 [8, 4, 2, 512, 512], P('energy', 'momentum')
- greater_new: bfloat16 [8, 4, 2, 512, 512], P('energy', 'momentum')
- retarded_new: bfloat16 [8, 4, 2, 512, 512], P('energy', 'momentum')
The draws below stay inside these ranges and needn't reach their ends.
Inputs may be any that keep to these rules, and one draw needn't show every extreme that they name: The energies of the grid are held in slots in an order of their own, one energy a slot. Mode m has one shift, the same for all slots: shift_slots[m, 0, j] is the slot of the energy that lies that shift below the energy of slot j, shift_slots[m, 1, j] the slot of the energy as far above it, and 8 where that energy lies outside the grid.
All inputs are finite; a program needn't handle non-finite values.
Results may differ from the reference program's by a relative error of at most 0.0064.
Values may be sent and summed in bfloat16 or wider, within the bound.
A program may use at most 64 MiB of HBM per device.

```python
import math
import jax
import jax.numpy as jnp
from jax import lax

B = 512
MODES = 2
ENERGIES = 8
MOMENTA = 4


def draw_shift_slots(key, part):
    order_key = jax.random.fold_in(key, 11)
    shift_key = jax.random.fold_in(key, 12)
    energy_of = jax.random.permutation(order_key, ENERGIES).astype(jnp.int32)
    slot_of = jnp.zeros((ENERGIES,), jnp.int32).at[energy_of].set(jnp.arange(ENERGIES, dtype=jnp.int32))
    shifts = jax.random.randint(shift_key, (MODES,), 1, ENERGIES // 2 + 1).astype(jnp.int32)
    below = energy_of[None, :] - shifts[:, None]
    above = energy_of[None, :] + shifts[:, None]
    below_slot = jnp.where(below >= 0, slot_of[jnp.clip(below, 0, ENERGIES - 1)], ENERGIES)
    above_slot = jnp.where(above < ENERGIES, slot_of[jnp.clip(above, 0, ENERGIES - 1)], ENERGIES)
    return jnp.stack([below_slot, above_slot], axis=1).astype(jnp.int32)


def touch_ends(entries, rng, least, high):
    extent = entries.shape
    index_at = [jax.random.randint(jax.random.fold_in(rng, axis), (), 0, extent[axis]) for axis in range(len(extent))]
    entries = entries.at[tuple(index_at)].set(least)
    longest = extent.index(max(extent))
    index_at[longest] = (index_at[longest] + 1) % extent[longest]
    return entries.at[tuple(index_at)].set(high)


def steps_of(own_key, shape, cuts, low, top_value):
    loudness, own = 1.0, jax.random.fold_in(own_key, 6)
    for position, parts in cuts:
        heights = jnp.exp(jax.random.uniform(jax.random.fold_in(own, position), (parts,), jnp.float32, low / len(cuts), top_value / len(cuts)))
        loudness = loudness * jnp.repeat(heights, shape[position] // parts).reshape([-1 if axis == position else 1 for axis in range(len(shape))])
    return loudness


def gaussian(key, dims, spread, reach, shards=(), held_as=jnp.bfloat16):
    values = spread * jax.random.normal(key, dims, jnp.float32)
    if shards:
        values = values * steps_of(key, dims, shards, -0.22, 0.18)
    return jnp.clip(values, -reach, reach).astype(held_as)


def setup_inputs(seed: int = 0) -> dict:
    key_list = jax.random.split(jax.random.key(seed), 7)
    return {
        "lesser": gaussian(key_list[0], (ENERGIES, MOMENTA, 2, B, B), 1.0, 6.0, ((0, 8), (1, 4))),
        "greater": gaussian(key_list[1], (ENERGIES, MOMENTA, 2, B, B), 1.0, 6.0, ((0, 8), (1, 4))),
        "retarded": gaussian(key_list[2], (ENERGIES, MOMENTA, 2, B, B), 0.7, 4.1875, ((0, 8), (1, 4))),
        "occupation": jnp.clip(jnp.exp(jax.random.uniform(key_list[3], (MODES,), jnp.float32, math.log(0.1), math.log(2.0))), 0.1, 2.0),
        "shift_slots": draw_shift_slots(jax.random.fold_in(key_list[6], 71), 0),
        "coupling": touch_ends(jax.random.randint(key_list[5], (MODES, MOMENTA, MOMENTA), 1, 9), jax.random.fold_in(key_list[5], 1), 1, 8).astype(jnp.int32),
    }


def matrix_product(former, latter):
    return jnp.matmul(former.astype(jnp.float32), latter.astype(jnp.float32), precision=lax.Precision.HIGHEST)


def complex_product(former, latter):
    former_re = former[..., 0, :, :]
    former_im = former[..., 1, :, :]
    latter_re = latter[..., 0, :, :]
    latter_im = latter[..., 1, :, :]
    real_part = matrix_product(former_re, latter_re) - matrix_product(former_im, latter_im)
    imag_part = matrix_product(former_re, latter_im) + matrix_product(former_im, latter_re)
    return jnp.stack([real_part, imag_part], axis=-3)


def adjoint_product(former, propagator):
    former_re = former[..., 0, :, :]
    former_im = former[..., 1, :, :]
    prop_re = jnp.swapaxes(propagator[..., 0, :, :], -1, -2)
    prop_im = jnp.swapaxes(propagator[..., 1, :, :], -1, -2)
    real_part = matrix_product(former_re, prop_re) + matrix_product(former_im, prop_im)
    imag_part = matrix_product(former_im, prop_re) - matrix_product(former_re, prop_im)
    return jnp.stack([real_part, imag_part], axis=-3)


def reference(lesser, greater, retarded, occupation, shift_slots, coupling):
    factor = 1.0 / (B * 4.0 * (MODES * MOMENTA) ** 0.5)
    filler = jnp.zeros((1, MOMENTA, 2, B, B), jnp.bfloat16)
    padded_less = jnp.concatenate([lesser, filler], axis=0)
    padded_more = jnp.concatenate([greater, filler], axis=0)
    weights = coupling.astype(jnp.float32)

    def one_slot(inputs):
        target, propagator = inputs
        total_less = jnp.zeros((MOMENTA, 2, B, B), jnp.float32)
        total_more = jnp.zeros((MOMENTA, 2, B, B), jnp.float32)
        for branch in range(MODES):
            phonons = occupation[branch]
            below_less = padded_less[shift_slots[branch, 0, target]].astype(jnp.float32)
            above_less = padded_less[shift_slots[branch, 1, target]].astype(jnp.float32)
            below_more = padded_more[shift_slots[branch, 0, target]].astype(jnp.float32)
            above_more = padded_more[shift_slots[branch, 1, target]].astype(jnp.float32)
            mix_less = phonons * below_less + (phonons + 1.0) * above_less
            mix_more = (phonons + 1.0) * below_more + phonons * above_more
            total_less = total_less + jnp.einsum("kq,qxab->kxab", weights[branch], mix_less, precision=lax.Precision.HIGHEST)
            total_more = total_more + jnp.einsum("kq,qxab->kxab", weights[branch], mix_more, precision=lax.Precision.HIGHEST)
        sigma_less = (total_less * factor).astype(jnp.bfloat16)
        sigma_more = (total_more * factor).astype(jnp.bfloat16)
        sigma_ret = ((sigma_more.astype(jnp.float32) - sigma_less.astype(jnp.float32)) * 0.5).astype(jnp.bfloat16)
        stacked = jnp.stack([sigma_less, sigma_more, sigma_ret])
        halfway = complex_product(propagator[None], stacked).astype(jnp.bfloat16)
        less_new = adjoint_product(halfway[0], propagator).astype(jnp.bfloat16)
        more_new = adjoint_product(halfway[1], propagator).astype(jnp.bfloat16)
        ret_new = (propagator.astype(jnp.float32) + complex_product(halfway[2], propagator)).astype(jnp.bfloat16)
        return less_new, more_new, ret_new

    targets = jnp.arange(ENERGIES, dtype=jnp.int32)
    lesser_new, greater_new, retarded_new = lax.map(one_slot, (targets, retarded))
    return (lesser_new, greater_new, retarded_new)
```

```python
import functools

import jax
import jax.numpy as jnp
from jax import lax
from jax.experimental import pallas as pl
from jax.experimental.pallas import tpu as pltpu
from jax.sharding import PartitionSpec as P

MESH = pl.DeviceIdType.MESH
STEP = 128
GRAIN = 2.0**27


def dot(a, b):
    return jnp.dot(a, b, preferred_element_type=jnp.float32)


def dot_t(a, b):
    return lax.dot_general(a, b, (((1,), (1,)), ((), ())), preferred_element_type=jnp.float32)


def products(ret, sigma, at, half_less, less_at, width):
    both = jnp.concatenate([sigma[0, :, at], sigma[1, :, at]], axis=1)
    by_re, by_im = dot(ret[0], both), dot(ret[1], both)
    more = by_re[:, :width] - by_im[:, width:], by_re[:, width:] + by_im[:, :width]
    wide = tuple((more[x] - half_less[x, :, less_at]) * 0.5 for x in range(2))
    return tuple(v.astype(jnp.bfloat16) for v in more), tuple(v.astype(jnp.bfloat16) for v in wide)


def adjoint_part(ret, half, at, to):
    re, im = half
    right = jnp.concatenate([ret[0, to, at], ret[1, to, at]], axis=1)
    return (
        dot_t(jnp.concatenate([re, im], axis=1), right),
        dot_t(jnp.concatenate([im, -re], axis=1), right),
    )


def dyson_part(ret, half, at, to):
    re, im = half
    right_re, right_im = ret[0, at, to], ret[1, at, to]
    return (
        dot(jnp.concatenate([re, -im], axis=1), jnp.concatenate([right_re, right_im], axis=0)),
        dot(jnp.concatenate([re, im], axis=1), jnp.concatenate([right_im, right_re], axis=0)),
    )


def kernel(sizes, factor, widths, tail, less_ref, more_ref, ret_ref, small_ref, *refs):
    energies, momenta, modes, parts, rows, cols, row_groups, col_groups = sizes
    stages = len(widths)
    less_new, ret_held, tail_less, tail_more, *refs = refs
    sum_more, sum_ret, refs = refs[:2], refs[2:4], refs[4:]
    small, recv_less, recv_more, mixed, send_less, sig_less, half, half_less, *refs = refs
    send_more, refs = refs[:stages], refs[stages:]
    sig_more, refs = refs[: stages - 1] + [tail_more], refs[stages - 1 :]
    send_sem, recv_sem, own_sem, load_sem, ready_sem = refs
    n = energies * momenta
    me = lax.axis_index("energy") * momenta + lax.axis_index("momentum")
    order = row_groups * rows
    bits = n.bit_length() - 1
    mine = [lax.rem(lax.div(me, 1 << b), 2) for b in range(bits)]

    def partner(d):
        other = 0
        for b in range(bits):
            flip = (d >> b) % 2 if isinstance(d, int) else lax.rem(lax.div(d, 1 << b), 2)
            other += (mine[b] + flip - 2 * mine[b] * flip) * (1 << b)
        return other

    def place(d):
        return lax.div(d, momenta), lax.rem(d, momenta)

    quarter = n // 4
    low = quarter.bit_length() - 1
    my_quarter = lax.div(me, quarter)
    my_half = lax.div(my_quarter, 2)
    far_half = 2 * (1 - my_half)
    near_quarter = 4 * my_half + 1 - my_quarter

    def others(act):
        def within(q, last):
            def at(t, carry):
                other = q * quarter
                for b in range(low):
                    flip = lax.rem(lax.div(quarter - 1 - t, 1 << b), 2)
                    other += (mine[b] + flip - 2 * mine[b] * flip) * (1 << b)
                act(other)
                return carry

            lax.fori_loop(0, last, at, 0)

        within(far_half, quarter)
        within(near_quarter, quarter)
        within(far_half + 1, quarter)
        within(my_quarter, quarter - 1)

    def piece(ref, lead, d, count):
        row = pl.multiple_of(lax.rem(d, row_groups) * rows, rows)
        rest = lax.div(d, row_groups)
        col = pl.multiple_of(lax.rem(rest, col_groups) * count, count)
        part = lax.div(rest, col_groups) * parts
        index = (pl.ds(part, parts), pl.ds(row, rows), pl.ds(col, count))
        return ref.at[(0,) * lead + index]

    def signal(sem, d):
        pl.semaphore_signal(sem, inc=1, device_id=place(d), device_id_type=MESH)

    barrier = pltpu.get_barrier_semaphore()
    for b in range(bits):
        signal(barrier, partner(1 << b))
    loads = [
        pltpu.make_async_copy(piece(less_ref, 2, me, cols), recv_less.at[me], own_sem.at[0]),
        pltpu.make_async_copy(piece(more_ref, 2, me, cols), recv_more.at[me], own_sem.at[1]),
        pltpu.make_async_copy(ret_ref.at[0, 0], ret_held, load_sem.at[0]),
        pltpu.make_async_copy(small_ref, small, load_sem.at[1]),
    ]
    for load in loads:
        load.start()

    def forward(ref, landing, which):
        def send(d):
            pltpu.make_async_remote_copy(
                src_ref=piece(ref, 2, d, cols),
                dst_ref=landing.at[me],
                send_sem=send_sem.at[which],
                recv_sem=recv_sem.at[which],
                device_id=place(d),
                device_id_type=MESH,
            ).start()

        return send

    def back(ref, landing, count, which):
        def send(d):
            pltpu.make_async_remote_copy(
                src_ref=ref.at[d],
                dst_ref=piece(landing, 0, me, count),
                send_sem=send_sem.at[which],
                recv_sem=recv_sem.at[which],
                device_id=place(d),
                device_id_type=MESH,
            ).start()

        others(send)

    def wait_all(sem, ref):
        span = ref.at[pl.ds(0, n - 1)]
        pltpu.make_async_copy(span, span, sem).wait()

    send = forward(less_ref, recv_less, 0)
    for level in range(bits):
        if level == 0:
            pl.semaphore_wait(barrier, bits)
        else:
            pl.semaphore_wait(ready_sem.at[level - 1], bits)
        if level < bits - 1:
            for b in range(bits):
                signal(ready_sem.at[level], partner(1 << b))
        for d in range(n - 1, 0, -1):
            if d.bit_count() == level + 1:
                send(partner(d))
    others(forward(more_ref, recv_more, 1))

    mixed[:, energies] = jnp.zeros((modes, momenta, parts, rows, cols), jnp.float32)

    def coupling(m, k, q):
        return small[m, k, q].astype(jnp.float32)

    def mix(recv, send, add_below, add_above, begin, count):
        step = min(count, max(4096 // rows, 128))
        blocks = parts * (count // step)

        def spot(i):
            b = lax.rem(i, blocks)
            col = lax.rem(b, count // step) * step
            return lax.div(i, blocks), lax.div(b, count // step), pl.multiple_of(col, step)

        def over_momenta(i, carry):
            s, part, col = spot(i)
            at = pl.ds(begin + col, step)
            terms = [recv[s * momenta + q, part, :, at].astype(jnp.float32) for q in range(momenta)]
            for m in range(modes):
                for k in range(momenta):
                    total = coupling(m, k, 0) * terms[0]
                    for q in range(1, momenta):
                        total += coupling(m, k, q) * terms[q]
                    mixed[m, s, k, part, :, at] = total
            return carry

        lax.fori_loop(0, energies * blocks, over_momenta, 0)

        def over_energies(i, carry):
            j, part, col = spot(i)
            at, to = pl.ds(begin + col, step), pl.ds(col, step)
            for k in range(momenta):
                total = None
                for m in range(modes):
                    phonons = small[m, momenta + 2, 0].astype(jnp.float32) * (1.0 / GRAIN)
                    for side, add in ((0, add_below), (1, add_above)):
                        slot = small[m, momenta + side, j]
                        term = ((phonons + add) * factor) * mixed[m, slot, k, part, :, at]
                        total = term if total is None else total + term
                send[j * momenta + k, part, :, to] = total.astype(jnp.bfloat16)
            return carry

        lax.fori_loop(0, energies * blocks, over_energies, 0)

    loads[3].wait()
    loads[0].wait()
    wait_all(recv_sem.at[0], recv_less)
    mix(recv_less, send_less, 0.0, 1.0, 0, cols)
    back(send_less, sig_less, cols, 2)
    keep_less = pltpu.make_async_copy(send_less.at[me], piece(sig_less, 0, me, cols), own_sem.at[0])
    keep_less.start()

    loads[1].wait()
    wait_all(recv_sem.at[1], recv_more)
    keeps, begin = [], 0
    for c, width in enumerate(widths):
        mix(recv_more, send_more[c], 1.0, 0.0, begin, width)
        back(send_more[c], sig_more[c], width, 3 + c)
        keep = pltpu.make_async_copy(send_more[c].at[me], piece(sig_more[c], 0, me, width), own_sem.at[1 + c])
        keep.start()
        keeps.append(keep)
        begin += width

    tile = min(order, 256)
    tiles = [pl.ds(t * tile, tile) for t in range(order // tile)]

    loads[2].wait()
    keep_less.wait()
    wait_all(recv_sem.at[2], send_less)
    for at in tiles:
        both_re, both_im = sig_less[0, :, at], sig_less[1, :, at]
        re = dot(ret_held[0], both_re) - dot(ret_held[1], both_im)
        im = dot(ret_held[0], both_im) + dot(ret_held[1], both_re)
        for x, value in enumerate((re, im)):
            half_less[x, :, at] = value
            half[x, :, at] = value.astype(jnp.bfloat16)
    tail_less[...] = half_less[:, :, tail:]
    for to in tiles:
        re, im, right_re, right_im = half[0], half[1], ret_held[0, to, :], ret_held[1, to, :]
        less_new[0, 0, 0, :, to] = (dot_t(re, right_re) + dot_t(im, right_im)).astype(jnp.bfloat16)
        less_new[0, 0, 1, :, to] = (dot_t(im, right_re) - dot_t(re, right_im)).astype(jnp.bfloat16)
    for x in range(2):
        for to in tiles:
            sum_ret[x][:, to] = ret_held[x, :, to].astype(jnp.float32)
            if tail == 0:
                sum_more[x][:, to] = jnp.zeros((order, tile), jnp.float32)

    begin = 0
    for c, width in enumerate(widths):
        keeps[c].wait()
        wait_all(recv_sem.at[3 + c], send_more[c])
        if begin < tail:
            for part in range(width // STEP):
                at = pl.ds(begin + part * STEP, STEP)
                more, wide = products(ret_held, sig_more[c], pl.ds(part * STEP, STEP), half_less, at, STEP)
                for to in tiles:
                    add_more, add_ret = adjoint_part(ret_held, more, at, to), dyson_part(ret_held, wide, at, to)
                    for x in range(2):
                        sum_ret[x][:, to] += add_ret[x]
                        if begin + part == 0:
                            sum_more[x][:, to] = add_more[x]
                        else:
                            sum_more[x][:, to] += add_more[x]
        begin += width
    for which, ref in enumerate([recv_less, recv_more, send_less, *send_more]):
        wait_all(send_sem.at[which], ref)


def finish(tail, less_new, ret_held, tail_less, tail_more, *refs):
    sum_more, sum_ret, refs = refs[:2], refs[2:4], refs[4:]
    less_out, more_out, ret_out, more_new, ret_new, sem = refs
    order = less_new.shape[-1]
    copies = [pltpu.make_async_copy(less_new, less_out, sem.at[0])]
    copies[0].start()
    tile = min(order, 256)
    steps = range(tail, order, STEP)
    halves = []
    for b in steps:
        at = pl.ds(b - tail, STEP)
        halves.append(products(ret_held, tail_more, at, tail_less, at, STEP))
    for t in range(order // tile):
        to = pl.ds(t * tile, tile)
        more, ret = [sum_more[x][:, to] for x in range(2)], [sum_ret[x][:, to] for x in range(2)]
        for b, (half_more, half_ret) in zip(steps, halves):
            add_more = adjoint_part(ret_held, half_more, pl.ds(b, STEP), to)
            add_ret = dyson_part(ret_held, half_ret, pl.ds(b, STEP), to)
            more = [more[x] + add_more[x] for x in range(2)]
            ret = [ret[x] + add_ret[x] for x in range(2)]
        for x in range(2):
            more_new[x, :, to] = more[x].astype(jnp.bfloat16)
            ret_new[x, :, to] = ret[x].astype(jnp.bfloat16)
        for i, (made, out) in enumerate(((more_new, more_out), (ret_new, ret_out))):
            copy = pltpu.make_async_copy(made.at[:, :, to], out.at[0, 0, :, :, to], sem.at[1 + 2 * t + i])
            copy.start()
            copies.append(copy)
    for copy in copies:
        copy.wait()


def per_device(energies, momenta, lesser, greater, retarded, occupation, shift_slots, coupling):
    n = energies * momenta
    modes = coupling.shape[0]
    order = lesser.shape[-1]
    factor = 1.0 / (order * 4.0 * (modes * momenta) ** 0.5)
    row_groups = min(n // 2, order // 16)
    col_groups = n // 2 // row_groups
    parts, rows, cols = 1, order // row_groups, order // col_groups
    sizes = (energies, momenta, modes, parts, rows, cols, row_groups, col_groups)
    vmem = pl.BlockSpec(memory_space=pltpu.VMEM)
    hbm = pl.BlockSpec(memory_space=pltpu.HBM)
    widths = (384, 128) if cols == 512 else (cols,)
    tail = order - widths[-1] if col_groups == 1 else 0
    stages = len(widths)

    def exchanged(width):
        return pltpu.VMEM((n, parts, rows, width), jnp.bfloat16)

    whole = pltpu.VMEM((2, order, order), jnp.bfloat16)
    new = jax.ShapeDtypeStruct(lesser.shape, jnp.bfloat16)
    total = jax.ShapeDtypeStruct((order, order), jnp.float32)
    length = max(energies, momenta)
    small = jnp.concatenate(
        [
            jnp.pad(coupling, ((0, 0), (0, 0), (0, length - momenta))),
            jnp.pad(shift_slots, ((0, 0), (0, 0), (0, length - energies))),
            jnp.broadcast_to((occupation * GRAIN).astype(jnp.int32)[:, None, None], (modes, 1, length)),
        ],
        axis=1,
    )
    held = pl.pallas_call(
        functools.partial(kernel, sizes, factor, widths, tail),
        out_shape=(
            new,
            jax.ShapeDtypeStruct((2, order, order), jnp.bfloat16),
            jax.ShapeDtypeStruct((2, order, order - tail), jnp.float32),
            jax.ShapeDtypeStruct((2, order, order - tail), jnp.bfloat16),
            *[total] * 4,
        ),
        in_specs=[hbm] * 4,
        out_specs=(vmem,) * 8,
        scratch_shapes=[
            pltpu.SMEM(small.shape, jnp.int32),
            exchanged(cols),
            exchanged(cols),
            pltpu.VMEM((modes, energies + 1, momenta, parts, rows, cols), jnp.float32),
            exchanged(cols),
            whole,
            whole,
            pltpu.VMEM((2, order, order), jnp.float32),
            *[exchanged(width) for width in widths],
            *[pltpu.VMEM((2, order, width * col_groups), jnp.bfloat16) for width in widths[:-1]],
            pltpu.SemaphoreType.DMA((3 + stages,)),
            pltpu.SemaphoreType.DMA((3 + stages,)),
            pltpu.SemaphoreType.DMA((1 + stages,)),
            pltpu.SemaphoreType.DMA((2,)),
            pltpu.SemaphoreType.REGULAR((n.bit_length() - 2,)),
        ],
        compiler_params=pltpu.CompilerParams(
            collective_id=0, has_side_effects=True, vmem_limit_bytes=47 * 1024 * 1024
        ),
        cost_estimate=pl.CostEstimate(
            flops=40 * order**3, bytes_accessed=24 * order * order, transcendentals=0
        ),
    )(lesser, greater, retarded, small)
    return pl.pallas_call(
        functools.partial(finish, tail),
        out_shape=(new, new, new),
        in_specs=[vmem] * 8,
        out_specs=(hbm,) * 3,
        scratch_shapes=[
            whole,
            whole,
            pltpu.SemaphoreType.DMA((1 + 2 * max(order // 256, 1),)),
        ],
        compiler_params=pltpu.CompilerParams(vmem_limit_bytes=16 * 1024 * 1024),
        cost_estimate=pl.CostEstimate(
            flops=8 * order**3, bytes_accessed=12 * order * order, transcendentals=0
        ),
    )(*held)


def solution(mesh):
    split = P("energy", "momentum", None, None, None)
    return jax.shard_map(
        functools.partial(per_device, mesh.shape["energy"], mesh.shape["momentum"]),
        mesh=mesh,
        in_specs=(split, split, split, P(), P(), P()),
        out_specs=(split, split, split),
        check_vma=False,
    )
```

```python
import functools

import jax
import jax.numpy as jnp
from jax import lax
from jax.experimental import pallas as pl
from jax.experimental.pallas import tpu as pltpu
from jax.sharding import PartitionSpec as P

MESH = pl.DeviceIdType.MESH
STEP = 128
GRAIN = 2.0**27


def dot(a, b):
    return jnp.dot(a, b, preferred_element_type=jnp.float32)


def dot_t(a, b):
    return lax.dot_general(a, b, (((1,), (1,)), ((), ())), preferred_element_type=jnp.float32)


def products(ret, sigma, at, half_less, less_at, width):
    both = jnp.concatenate([sigma[0, :, at], sigma[1, :, at]], axis=1)
    by_re, by_im = dot(ret[0], both), dot(ret[1], both)
    more = by_re[:, :width] - by_im[:, width:], by_re[:, width:] + by_im[:, :width]
    wide = tuple((more[x] - half_less[x, :, less_at]) * 0.5 for x in range(2))
    return tuple(v.astype(jnp.bfloat16) for v in more), tuple(v.astype(jnp.bfloat16) for v in wide)


def adjoint_part(ret, half, at, to):
    re, im = half
    right = jnp.concatenate([ret[0, to, at], ret[1, to, at]], axis=1)
    return (
        dot_t(jnp.concatenate([re, im], axis=1), right),
        dot_t(jnp.concatenate([im, -re], axis=1), right),
    )


def dyson_part(ret, half, at, to):
    re, im = half
    right_re, right_im = ret[0, at, to], ret[1, at, to]
    return (
        dot(jnp.concatenate([re, -im], axis=1), jnp.concatenate([right_re, right_im], axis=0)),
        dot(jnp.concatenate([re, im], axis=1), jnp.concatenate([right_im, right_re], axis=0)),
    )


def kernel(sizes, factor, widths, tail, less_ref, more_ref, ret_ref, small_ref, *refs):
    energies, momenta, modes, parts, rows, cols, row_groups, col_groups = sizes
    stages = len(widths)
    less_new, ret_held, tail_less, tail_more, *refs = refs
    sum_more, sum_ret, refs = refs[:2], refs[2:4], refs[4:]
    small, recv_less, recv_more, mixed, send_less, sig_less, half, half_less, *refs = refs
    send_more, refs = refs[:stages], refs[stages:]
    sig_more, refs = refs[: stages - 1] + [tail_more], refs[stages - 1 :]
    send_sem, recv_sem, own_sem, load_sem, ready_sem = refs
    n = energies * momenta
    me = lax.axis_index("energy") * momenta + lax.axis_index("momentum")
    order = row_groups * rows
    bits = n.bit_length() - 1
    mine = [lax.rem(lax.div(me, 1 << b), 2) for b in range(bits)]

    def partner(d):
        other = 0
        for b in range(bits):
            flip = (d >> b) % 2 if isinstance(d, int) else lax.rem(lax.div(d, 1 << b), 2)
            other += (mine[b] + flip - 2 * mine[b] * flip) * (1 << b)
        return other

    def place(d):
        return lax.div(d, momenta), lax.rem(d, momenta)

    quarter = n // 4
    low = quarter.bit_length() - 1
    my_quarter = lax.div(me, quarter)
    my_half = lax.div(my_quarter, 2)
    far_half = 2 * (1 - my_half)
    near_quarter = 4 * my_half + 1 - my_quarter

    def others(act, ending=False):
        def target(q, t, fixed):
            if fixed:
                return q * quarter + t
            other = q * quarter
            for b in range(low):
                flip = lax.rem(lax.div(quarter - 1 - t, 1 << b), 2)
                other += (mine[b] + flip - 2 * mine[b] * flip) * (1 << b)
            return other

        def blend(quarters, fixed):
            def at(t, carry):
                for q in quarters:
                    act(target(q, t, fixed))
                return carry

            lax.fori_loop(0, quarter, at, 0)

        def own(t, carry):
            act(target(my_quarter, t, False))
            return carry

        if ending:
            blend([far_half], True)
            blend([near_quarter], True)
            blend([far_half + 1], True)
            lax.fori_loop(0, quarter - 1, own, 0)
        else:
            blend([far_half], False)
            blend([near_quarter], False)
            blend([far_half + 1], False)
            lax.fori_loop(0, quarter - 1, own, 0)

    def piece(ref, lead, d, count):
        row = pl.multiple_of(lax.rem(d, row_groups) * rows, rows)
        rest = lax.div(d, row_groups)
        col = pl.multiple_of(lax.rem(rest, col_groups) * count, count)
        part = lax.div(rest, col_groups) * parts
        index = (pl.ds(part, parts), pl.ds(row, rows), pl.ds(col, count))
        return ref.at[(0,) * lead + index]

    def signal(sem, d):
        pl.semaphore_signal(sem, inc=1, device_id=place(d), device_id_type=MESH)

    barrier = pltpu.get_barrier_semaphore()
    for b in range(bits):
        signal(barrier, partner(1 << b))
    loads = [
        pltpu.make_async_copy(piece(less_ref, 2, me, cols), recv_less.at[me], own_sem.at[0]),
        pltpu.make_async_copy(piece(more_ref, 2, me, cols), recv_more.at[me], own_sem.at[1]),
        pltpu.make_async_copy(ret_ref.at[0, 0], ret_held, load_sem.at[0]),
        pltpu.make_async_copy(small_ref, small, load_sem.at[1]),
    ]
    for load in loads:
        load.start()

    def forward(ref, landing, which):
        def send(d):
            pltpu.make_async_remote_copy(
                src_ref=piece(ref, 2, d, cols),
                dst_ref=landing.at[me],
                send_sem=send_sem.at[which],
                recv_sem=recv_sem.at[which],
                device_id=place(d),
                device_id_type=MESH,
            ).start()

        return send

    def back(ref, landing, count, which, ending=False):
        def send(d):
            pltpu.make_async_remote_copy(
                src_ref=ref.at[d],
                dst_ref=piece(landing, 0, me, count),
                send_sem=send_sem.at[which],
                recv_sem=recv_sem.at[which],
                device_id=place(d),
                device_id_type=MESH,
            ).start()

        others(send, ending)

    def wait_all(sem, ref):
        span = ref.at[pl.ds(0, n - 1)]
        pltpu.make_async_copy(span, span, sem).wait()

    send = forward(less_ref, recv_less, 0)
    for level in range(bits):
        if level == 0:
            pl.semaphore_wait(barrier, bits)
        else:
            pl.semaphore_wait(ready_sem.at[level - 1], bits)
        if level < bits - 1:
            for b in range(bits):
                signal(ready_sem.at[level], partner(1 << b))
        for d in range(n - 1, 0, -1):
            if d.bit_count() == level + 1:
                send(partner(d))
    others(forward(more_ref, recv_more, 1))

    mixed[:, energies] = jnp.zeros((modes, momenta, parts, rows, cols), jnp.float32)

    def coupling(m, k, q):
        return small[m, k, q].astype(jnp.float32)

    def mix(recv, send, add_below, add_above, begin, count):
        step = min(count, max(4096 // rows, 128))
        blocks = parts * (count // step)

        def spot(i):
            b = lax.rem(i, blocks)
            col = lax.rem(b, count // step) * step
            return lax.div(i, blocks), lax.div(b, count // step), pl.multiple_of(col, step)

        def over_momenta(i, carry):
            s, part, col = spot(i)
            at = pl.ds(begin + col, step)
            terms = [recv[s * momenta + q, part, :, at].astype(jnp.float32) for q in range(momenta)]
            for m in range(modes):
                for k in range(momenta):
                    total = coupling(m, k, 0) * terms[0]
                    for q in range(1, momenta):
                        total += coupling(m, k, q) * terms[q]
                    mixed[m, s, k, part, :, at] = total
            return carry

        lax.fori_loop(0, energies * blocks, over_momenta, 0)

        def over_energies(i, carry):
            j, part, col = spot(i)
            at, to = pl.ds(begin + col, step), pl.ds(col, step)
            for k in range(momenta):
                total = None
                for m in range(modes):
                    phonons = small[m, momenta + 2, 0].astype(jnp.float32) * (1.0 / GRAIN)
                    for side, add in ((0, add_below), (1, add_above)):
                        slot = small[m, momenta + side, j]
                        term = ((phonons + add) * factor) * mixed[m, slot, k, part, :, at]
                        total = term if total is None else total + term
                send[j * momenta + k, part, :, to] = total.astype(jnp.bfloat16)
            return carry

        lax.fori_loop(0, energies * blocks, over_energies, 0)

    loads[3].wait()
    loads[0].wait()
    wait_all(recv_sem.at[0], recv_less)
    mix(recv_less, send_less, 0.0, 1.0, 0, cols)
    back(send_less, sig_less, cols, 2)
    keep_less = pltpu.make_async_copy(send_less.at[me], piece(sig_less, 0, me, cols), own_sem.at[0])
    keep_less.start()

    loads[1].wait()
    wait_all(recv_sem.at[1], recv_more)
    keeps, begin = [], 0
    for c, width in enumerate(widths):
        mix(recv_more, send_more[c], 1.0, 0.0, begin, width)
        back(send_more[c], sig_more[c], width, 3 + c, c == stages - 1)
        keep = pltpu.make_async_copy(send_more[c].at[me], piece(sig_more[c], 0, me, width), own_sem.at[1 + c])
        keep.start()
        keeps.append(keep)
        begin += width

    tile = min(order, 256)
    tiles = [pl.ds(t * tile, tile) for t in range(order // tile)]

    loads[2].wait()
    keep_less.wait()
    wait_all(recv_sem.at[2], send_less)
    for at in tiles:
        both_re, both_im = sig_less[0, :, at], sig_less[1, :, at]
        re = dot(ret_held[0], both_re) - dot(ret_held[1], both_im)
        im = dot(ret_held[0], both_im) + dot(ret_held[1], both_re)
        for x, value in enumerate((re, im)):
            half_less[x, :, at] = value
            half[x, :, at] = value.astype(jnp.bfloat16)
    tail_less[...] = half_less[:, :, tail:]
    for to in tiles:
        re, im, right_re, right_im = half[0], half[1], ret_held[0, to, :], ret_held[1, to, :]
        less_new[0, 0, 0, :, to] = (dot_t(re, right_re) + dot_t(im, right_im)).astype(jnp.bfloat16)
        less_new[0, 0, 1, :, to] = (dot_t(im, right_re) - dot_t(re, right_im)).astype(jnp.bfloat16)
    for x in range(2):
        for to in tiles:
            sum_ret[x][:, to] = ret_held[x, :, to].astype(jnp.float32)
            if tail == 0:
                sum_more[x][:, to] = jnp.zeros((order, tile), jnp.float32)

    begin = 0
    for c, width in enumerate(widths):
        keeps[c].wait()
        wait_all(recv_sem.at[3 + c], send_more[c])
        if begin < tail:
            for part in range(width // STEP):
                at = pl.ds(begin + part * STEP, STEP)
                more, wide = products(ret_held, sig_more[c], pl.ds(part * STEP, STEP), half_less, at, STEP)
                for to in tiles:
                    add_more, add_ret = adjoint_part(ret_held, more, at, to), dyson_part(ret_held, wide, at, to)
                    for x in range(2):
                        sum_ret[x][:, to] += add_ret[x]
                        if begin + part == 0:
                            sum_more[x][:, to] = add_more[x]
                        else:
                            sum_more[x][:, to] += add_more[x]
        begin += width
    for which, ref in enumerate([recv_less, recv_more, send_less, *send_more]):
        wait_all(send_sem.at[which], ref)


def finish(tail, less_new, ret_held, tail_less, tail_more, *refs):
    sum_more, sum_ret, refs = refs[:2], refs[2:4], refs[4:]
    less_out, more_out, ret_out, more_new, ret_new, sem = refs
    order = less_new.shape[-1]
    copies = [pltpu.make_async_copy(less_new, less_out, sem.at[0])]
    copies[0].start()
    tile = min(order, 256)
    steps = range(tail, order, STEP)
    halves = []
    for b in steps:
        at = pl.ds(b - tail, STEP)
        halves.append(products(ret_held, tail_more, at, tail_less, at, STEP))
    for t in range(order // tile):
        to = pl.ds(t * tile, tile)
        more, ret = [sum_more[x][:, to] for x in range(2)], [sum_ret[x][:, to] for x in range(2)]
        for b, (half_more, half_ret) in zip(steps, halves):
            add_more = adjoint_part(ret_held, half_more, pl.ds(b, STEP), to)
            add_ret = dyson_part(ret_held, half_ret, pl.ds(b, STEP), to)
            more = [more[x] + add_more[x] for x in range(2)]
            ret = [ret[x] + add_ret[x] for x in range(2)]
        for x in range(2):
            more_new[x, :, to] = more[x].astype(jnp.bfloat16)
            ret_new[x, :, to] = ret[x].astype(jnp.bfloat16)
        for i, (made, out) in enumerate(((more_new, more_out), (ret_new, ret_out))):
            copy = pltpu.make_async_copy(made.at[:, :, to], out.at[0, 0, :, :, to], sem.at[1 + 2 * t + i])
            copy.start()
            copies.append(copy)
    for copy in copies:
        copy.wait()


def per_device(energies, momenta, lesser, greater, retarded, occupation, shift_slots, coupling):
    n = energies * momenta
    modes = coupling.shape[0]
    order = lesser.shape[-1]
    factor = 1.0 / (order * 4.0 * (modes * momenta) ** 0.5)
    row_groups = min(n // 2, order // 16)
    col_groups = n // 2 // row_groups
    parts, rows, cols = 1, order // row_groups, order // col_groups
    sizes = (energies, momenta, modes, parts, rows, cols, row_groups, col_groups)
    vmem = pl.BlockSpec(memory_space=pltpu.VMEM)
    hbm = pl.BlockSpec(memory_space=pltpu.HBM)
    widths = (384, 128) if cols == 512 else (cols,)
    tail = order - widths[-1] if col_groups == 1 else 0
    stages = len(widths)

    def exchanged(width):
        return pltpu.VMEM((n, parts, rows, width), jnp.bfloat16)

    whole = pltpu.VMEM((2, order, order), jnp.bfloat16)
    new = jax.ShapeDtypeStruct(lesser.shape, jnp.bfloat16)
    total = jax.ShapeDtypeStruct((order, order), jnp.float32)
    length = max(energies, momenta)
    packed = (modes, momenta + 3, length)
    row = lax.broadcasted_iota(jnp.int32, packed, 1)
    grains = (lax.broadcast_in_dim(occupation, packed, (0,)) * GRAIN).astype(jnp.int32)
    weights = lax.pad(coupling, 0, ((0, 0, 0), (0, 3, 0), (0, length - momenta, 0)))
    slots = lax.pad(shift_slots, 0, ((0, 0, 0), (momenta, 1, 0), (0, length - energies, 0)))
    small = jnp.where(row == momenta + 2, grains, weights + slots)
    held = pl.pallas_call(
        functools.partial(kernel, sizes, factor, widths, tail),
        out_shape=(
            new,
            jax.ShapeDtypeStruct((2, order, order), jnp.bfloat16),
            jax.ShapeDtypeStruct((2, order, order - tail), jnp.float32),
            jax.ShapeDtypeStruct((2, order, order - tail), jnp.bfloat16),
            *[total] * 4,
        ),
        in_specs=[hbm] * 4,
        out_specs=(vmem,) * 8,
        scratch_shapes=[
            pltpu.SMEM(small.shape, jnp.int32),
            exchanged(cols),
            exchanged(cols),
            pltpu.VMEM((modes, energies + 1, momenta, parts, rows, cols), jnp.float32),
            exchanged(cols),
            whole,
            whole,
            pltpu.VMEM((2, order, order), jnp.float32),
            *[exchanged(width) for width in widths],
            *[pltpu.VMEM((2, order, width * col_groups), jnp.bfloat16) for width in widths[:-1]],
            pltpu.SemaphoreType.DMA((3 + stages,)),
            pltpu.SemaphoreType.DMA((3 + stages,)),
            pltpu.SemaphoreType.DMA((1 + stages,)),
            pltpu.SemaphoreType.DMA((2,)),
            pltpu.SemaphoreType.REGULAR((n.bit_length() - 2,)),
        ],
        compiler_params=pltpu.CompilerParams(
            collective_id=0, has_side_effects=True, vmem_limit_bytes=47 * 1024 * 1024
        ),
        cost_estimate=pl.CostEstimate(
            flops=40 * order**3, bytes_accessed=24 * order * order, transcendentals=0
        ),
    )(lesser, greater, retarded, small)
    return pl.pallas_call(
        functools.partial(finish, tail),
        out_shape=(new, new, new),
        in_specs=[vmem] * 8,
        out_specs=(hbm,) * 3,
        scratch_shapes=[
            whole,
            whole,
            pltpu.SemaphoreType.DMA((1 + 2 * max(order // 256, 1),)),
        ],
        compiler_params=pltpu.CompilerParams(vmem_limit_bytes=16 * 1024 * 1024),
        cost_estimate=pl.CostEstimate(
            flops=8 * order**3, bytes_accessed=12 * order * order, transcendentals=0
        ),
    )(*held)


def solution(mesh):
    split = P("energy", "momentum", None, None, None)
    return jax.shard_map(
        functools.partial(per_device, mesh.shape["energy"], mesh.shape["momentum"]),
        mesh=mesh,
        in_specs=(split, split, split, P(), P(), P()),
        out_specs=(split, split, split),
        check_vma=False,
    )
```

```python
import functools

import jax
import jax.numpy as jnp
from jax import lax
from jax.experimental import pallas as pl
from jax.experimental.pallas import tpu as pltpu
from jax.sharding import PartitionSpec as P

MESH = pl.DeviceIdType.MESH
STEP = 128
GRAIN = 2.0**27


def dot(a, b):
    return jnp.dot(a, b, preferred_element_type=jnp.float32)


def dot_t(a, b):
    return lax.dot_general(a, b, (((1,), (1,)), ((), ())), preferred_element_type=jnp.float32)


def products(ret, sigma, at, half_less, less_at, width):
    both = jnp.concatenate([sigma[0, :, at], sigma[1, :, at]], axis=1)
    by_re, by_im = dot(ret[0], both), dot(ret[1], both)
    more = by_re[:, :width] - by_im[:, width:], by_re[:, width:] + by_im[:, :width]
    wide = tuple((more[x] - half_less[x, :, less_at]) * 0.5 for x in range(2))
    return tuple(v.astype(jnp.bfloat16) for v in more), tuple(v.astype(jnp.bfloat16) for v in wide)


def adjoint_part(ret, half, at, to):
    re, im = half
    right = jnp.concatenate([ret[0, to, at], ret[1, to, at]], axis=1)
    return (
        dot_t(jnp.concatenate([re, im], axis=1), right),
        dot_t(jnp.concatenate([im, -re], axis=1), right),
    )


def dyson_part(ret, half, at, to):
    re, im = half
    right_re, right_im = ret[0, at, to], ret[1, at, to]
    return (
        dot(jnp.concatenate([re, -im], axis=1), jnp.concatenate([right_re, right_im], axis=0)),
        dot(jnp.concatenate([re, im], axis=1), jnp.concatenate([right_im, right_re], axis=0)),
    )


def kernel(sizes, factor, widths, tail, less_ref, more_ref, ret_ref, small_ref, *refs):
    energies, momenta, modes, parts, rows, cols, row_groups, col_groups = sizes
    stages = len(widths)
    less_new, ret_held, tail_less, tail_more, *refs = refs
    sum_more, sum_ret, refs = refs[:2], refs[2:4], refs[4:]
    small, recv_less, recv_more, mixed, send_less, sig_less, half, half_less, *refs = refs
    send_more, refs = refs[:stages], refs[stages:]
    sig_more, refs = refs[: stages - 1] + [tail_more], refs[stages - 1 :]
    send_sem, recv_sem, own_sem, load_sem, ready_sem = refs
    n = energies * momenta
    me = lax.axis_index("energy") * momenta + lax.axis_index("momentum")
    order = row_groups * rows
    bits = n.bit_length() - 1
    mine = [lax.rem(lax.div(me, 1 << b), 2) for b in range(bits)]

    def partner(d):
        other = 0
        for b in range(bits):
            flip = (d >> b) % 2 if isinstance(d, int) else lax.rem(lax.div(d, 1 << b), 2)
            other += (mine[b] + flip - 2 * mine[b] * flip) * (1 << b)
        return other

    def place(d):
        return lax.div(d, momenta), lax.rem(d, momenta)

    quarter = n // 4
    low = quarter.bit_length() - 1
    my_quarter = lax.div(me, quarter)
    my_half = lax.div(my_quarter, 2)
    far_half = 2 * (1 - my_half)
    near_quarter = 4 * my_half + 1 - my_quarter

    def others(act, ending=False, first=True, which=("low", "high")):
        def target(q, t, fixed):
            if fixed:
                return q * quarter + t
            other = q * quarter
            for b in range(low):
                flip = lax.rem(lax.div(quarter - 1 - t, 1 << b), 2)
                other += (mine[b] + flip - 2 * mine[b] * flip) * (1 << b)
            return other

        def blend(quarters, fixed, skip=0):
            def at(t, carry):
                for q in quarters:
                    act(target(q, t, fixed))
                return carry

            lax.fori_loop(0, quarter - skip, at, 0)

        def own(t, carry):
            act(target(my_quarter, t, False))
            return carry

        skip = 0 if first else 1
        if skip:
            act((far_half + 1 - lax.rem(my_quarter, 2)) * quarter + lax.rem(me, quarter))
        if "low" in which:
            blend([far_half], ending, skip)
            blend([near_quarter], ending)
        if "high" in which:
            blend([far_half + 1], ending, skip)
            lax.fori_loop(0, quarter - 1, own, 0)

    def piece(ref, lead, d, count):
        row = pl.multiple_of(lax.rem(d, row_groups) * rows, rows)
        rest = lax.div(d, row_groups)
        col = pl.multiple_of(lax.rem(rest, col_groups) * count, count)
        part = lax.div(rest, col_groups) * parts
        index = (pl.ds(part, parts), pl.ds(row, rows), pl.ds(col, count))
        return ref.at[(0,) * lead + index]

    def signal(sem, d):
        pl.semaphore_signal(sem, inc=1, device_id=place(d), device_id_type=MESH)

    barrier = pltpu.get_barrier_semaphore()
    for b in range(bits):
        signal(barrier, partner(1 << b))
    loads = [
        pltpu.make_async_copy(piece(less_ref, 2, me, cols), recv_less.at[me], own_sem.at[0]),
        pltpu.make_async_copy(piece(more_ref, 2, me, cols), recv_more.at[me], own_sem.at[1]),
        pltpu.make_async_copy(ret_ref.at[0, 0], ret_held, load_sem.at[0]),
        pltpu.make_async_copy(small_ref, small, load_sem.at[1]),
    ]
    for load in loads:
        load.start()

    def forward(ref, landing, which):
        def send(d):
            pltpu.make_async_remote_copy(
                src_ref=piece(ref, 2, d, cols),
                dst_ref=landing.at[me],
                send_sem=send_sem.at[which],
                recv_sem=recv_sem.at[which],
                device_id=place(d),
                device_id_type=MESH,
            ).start()

        return send

    def back(ref, landing, count, which, ending=False, targets=("low", "high")):
        def send(d):
            pltpu.make_async_remote_copy(
                src_ref=ref.at[d],
                dst_ref=piece(landing, 0, me, count),
                send_sem=send_sem.at[which],
                recv_sem=recv_sem.at[which],
                device_id=place(d),
                device_id_type=MESH,
            ).start()

        others(send, ending, which=targets)

    def wait_all(sem, ref):
        span = ref.at[pl.ds(0, n - 1)]
        pltpu.make_async_copy(span, span, sem).wait()

    send = forward(less_ref, recv_less, 0)
    send_more_forward = forward(more_ref, recv_more, 1)
    for level in range(bits):
        if level == 0:
            pl.semaphore_wait(barrier, bits)
        else:
            pl.semaphore_wait(ready_sem.at[level - 1], bits)
        if level < bits - 1:
            for b in range(bits):
                signal(ready_sem.at[level], partner(1 << b))
        for d in range(n - 1, 0, -1):
            if d.bit_count() == level + 1:
                send(partner(d))
                if d == n // 2:
                    send_more_forward(partner(d))
    others(send_more_forward, first=False)

    mixed[:, energies] = jnp.zeros((modes, momenta, parts, rows, cols), jnp.float32)

    def coupling(m, k, q):
        return small[m, k, q].astype(jnp.float32)

    def mix(recv, send, add_below, add_above, begin, count):
        step = min(count, max(4096 // rows, 128))
        blocks = parts * (count // step)

        def spot(i):
            b = lax.rem(i, blocks)
            col = lax.rem(b, count // step) * step
            return lax.div(i, blocks), lax.div(b, count // step), pl.multiple_of(col, step)

        def over_momenta(i, carry):
            s, part, col = spot(i)
            at = pl.ds(begin + col, step)
            terms = [recv[s * momenta + q, part, :, at].astype(jnp.float32) for q in range(momenta)]
            for m in range(modes):
                for k in range(momenta):
                    total = coupling(m, k, 0) * terms[0]
                    for q in range(1, momenta):
                        total += coupling(m, k, q) * terms[q]
                    mixed[m, s, k, part, :, at] = total
            return carry

        lax.fori_loop(0, energies * blocks, over_momenta, 0)

        def over_energies(i, carry):
            j, part, col = spot(i)
            at, to = pl.ds(begin + col, step), pl.ds(col, step)
            for k in range(momenta):
                total = None
                for m in range(modes):
                    phonons = small[m, momenta + 2, 0].astype(jnp.float32) * (1.0 / GRAIN)
                    for side, add in ((0, add_below), (1, add_above)):
                        slot = small[m, momenta + side, j]
                        term = ((phonons + add) * factor) * mixed[m, slot, k, part, :, at]
                        total = term if total is None else total + term
                send[j * momenta + k, part, :, to] = total.astype(jnp.bfloat16)
            return carry

        lax.fori_loop(0, energies * blocks, over_energies, 0)

    loads[3].wait()
    loads[0].wait()
    wait_all(recv_sem.at[0], recv_less)
    mix(recv_less, send_less, 0.0, 1.0, 0, cols)
    back(send_less, sig_less, cols, 2)
    keep_less = pltpu.make_async_copy(send_less.at[me], piece(sig_less, 0, me, cols), own_sem.at[0])
    keep_less.start()

    loads[1].wait()
    wait_all(recv_sem.at[1], recv_more)
    keeps, begin = [], 0
    for c, width in enumerate(widths):
        mix(recv_more, send_more[c], 1.0, 0.0, begin, width)
        back(send_more[c], sig_more[c], width, 3 + c, c == stages - 1, ("low",))
        keep = pltpu.make_async_copy(send_more[c].at[me], piece(sig_more[c], 0, me, width), own_sem.at[1 + c])
        keep.start()
        keeps.append(keep)
        begin += width
    for c, width in enumerate(widths):
        back(send_more[c], sig_more[c], width, 3 + c, c == stages - 1, ("high",))

    tile = min(order, 256)
    tiles = [pl.ds(t * tile, tile) for t in range(order // tile)]

    loads[2].wait()
    keep_less.wait()
    wait_all(recv_sem.at[2], send_less)
    for at in tiles:
        both_re, both_im = sig_less[0, :, at], sig_less[1, :, at]
        re = dot(ret_held[0], both_re) - dot(ret_held[1], both_im)
        im = dot(ret_held[0], both_im) + dot(ret_held[1], both_re)
        for x, value in enumerate((re, im)):
            half_less[x, :, at] = value
            half[x, :, at] = value.astype(jnp.bfloat16)
    tail_less[...] = half_less[:, :, tail:]
    for to in tiles:
        re, im, right_re, right_im = half[0], half[1], ret_held[0, to, :], ret_held[1, to, :]
        less_new[0, 0, 0, :, to] = (dot_t(re, right_re) + dot_t(im, right_im)).astype(jnp.bfloat16)
        less_new[0, 0, 1, :, to] = (dot_t(im, right_re) - dot_t(re, right_im)).astype(jnp.bfloat16)
    for x in range(2):
        for to in tiles:
            sum_ret[x][:, to] = ret_held[x, :, to].astype(jnp.float32)
            if tail == 0:
                sum_more[x][:, to] = jnp.zeros((order, tile), jnp.float32)

    begin = 0
    for c, width in enumerate(widths):
        keeps[c].wait()
        wait_all(recv_sem.at[3 + c], send_more[c])
        if begin < tail:
            for part in range(width // STEP):
                at = pl.ds(begin + part * STEP, STEP)
                more, wide = products(ret_held, sig_more[c], pl.ds(part * STEP, STEP), half_less, at, STEP)
                for to in tiles:
                    add_more, add_ret = adjoint_part(ret_held, more, at, to), dyson_part(ret_held, wide, at, to)
                    for x in range(2):
                        sum_ret[x][:, to] += add_ret[x]
                        if begin + part == 0:
                            sum_more[x][:, to] = add_more[x]
                        else:
                            sum_more[x][:, to] += add_more[x]
        begin += width
    for which, ref in enumerate([recv_less, recv_more, send_less, *send_more]):
        wait_all(send_sem.at[which], ref)


def finish(tail, less_new, ret_held, tail_less, tail_more, *refs):
    sum_more, sum_ret, refs = refs[:2], refs[2:4], refs[4:]
    less_out, more_out, ret_out, more_new, ret_new, sem = refs
    order = less_new.shape[-1]
    copies = [pltpu.make_async_copy(less_new, less_out, sem.at[0])]
    copies[0].start()
    tile = min(order, 256)
    steps = range(tail, order, STEP)
    halves = []
    for b in steps:
        at = pl.ds(b - tail, STEP)
        halves.append(products(ret_held, tail_more, at, tail_less, at, STEP))
    for t in range(order // tile):
        to = pl.ds(t * tile, tile)
        more, ret = [sum_more[x][:, to] for x in range(2)], [sum_ret[x][:, to] for x in range(2)]
        for b, (half_more, half_ret) in zip(steps, halves):
            add_more = adjoint_part(ret_held, half_more, pl.ds(b, STEP), to)
            add_ret = dyson_part(ret_held, half_ret, pl.ds(b, STEP), to)
            more = [more[x] + add_more[x] for x in range(2)]
            ret = [ret[x] + add_ret[x] for x in range(2)]
        for x in range(2):
            more_new[x, :, to] = more[x].astype(jnp.bfloat16)
            ret_new[x, :, to] = ret[x].astype(jnp.bfloat16)
        for i, (made, out) in enumerate(((more_new, more_out), (ret_new, ret_out))):
            copy = pltpu.make_async_copy(made.at[:, :, to], out.at[0, 0, :, :, to], sem.at[1 + 2 * t + i])
            copy.start()
            copies.append(copy)
    for copy in copies:
        copy.wait()


def per_device(energies, momenta, lesser, greater, retarded, occupation, shift_slots, coupling):
    n = energies * momenta
    modes = coupling.shape[0]
    order = lesser.shape[-1]
    factor = 1.0 / (order * 4.0 * (modes * momenta) ** 0.5)
    row_groups = min(n // 2, order // 16)
    col_groups = n // 2 // row_groups
    parts, rows, cols = 1, order // row_groups, order // col_groups
    sizes = (energies, momenta, modes, parts, rows, cols, row_groups, col_groups)
    vmem = pl.BlockSpec(memory_space=pltpu.VMEM)
    hbm = pl.BlockSpec(memory_space=pltpu.HBM)
    widths = (128, 128, 128, 128) if cols == 512 else (cols,)
    tail = order - widths[-1] if col_groups == 1 else 0
    stages = len(widths)

    def exchanged(width):
        return pltpu.VMEM((n, parts, rows, width), jnp.bfloat16)

    whole = pltpu.VMEM((2, order, order), jnp.bfloat16)
    new = jax.ShapeDtypeStruct(lesser.shape, jnp.bfloat16)
    total = jax.ShapeDtypeStruct((order, order), jnp.float32)
    length = max(energies, momenta)
    packed = (modes, momenta + 3, length)
    row = lax.broadcasted_iota(jnp.int32, packed, 1)
    grains = (lax.broadcast_in_dim(occupation, packed, (0,)) * GRAIN).astype(jnp.int32)
    weights = lax.pad(coupling, 0, ((0, 0, 0), (0, 3, 0), (0, length - momenta, 0)))
    slots = lax.pad(shift_slots, 0, ((0, 0, 0), (momenta, 1, 0), (0, length - energies, 0)))
    small = jnp.where(row == momenta + 2, grains, weights + slots)
    held = pl.pallas_call(
        functools.partial(kernel, sizes, factor, widths, tail),
        out_shape=(
            new,
            jax.ShapeDtypeStruct((2, order, order), jnp.bfloat16),
            jax.ShapeDtypeStruct((2, order, order - tail), jnp.float32),
            jax.ShapeDtypeStruct((2, order, order - tail), jnp.bfloat16),
            *[total] * 4,
        ),
        in_specs=[hbm] * 4,
        out_specs=(vmem,) * 8,
        scratch_shapes=[
            pltpu.SMEM(small.shape, jnp.int32),
            exchanged(cols),
            exchanged(cols),
            pltpu.VMEM((modes, energies + 1, momenta, parts, rows, cols), jnp.float32),
            exchanged(cols),
            whole,
            whole,
            pltpu.VMEM((2, order, order), jnp.float32),
            *[exchanged(width) for width in widths],
            *[pltpu.VMEM((2, order, width * col_groups), jnp.bfloat16) for width in widths[:-1]],
            pltpu.SemaphoreType.DMA((3 + stages,)),
            pltpu.SemaphoreType.DMA((3 + stages,)),
            pltpu.SemaphoreType.DMA((1 + stages,)),
            pltpu.SemaphoreType.DMA((2,)),
            pltpu.SemaphoreType.REGULAR((n.bit_length() - 2,)),
        ],
        compiler_params=pltpu.CompilerParams(
            collective_id=0, has_side_effects=True, vmem_limit_bytes=47 * 1024 * 1024
        ),
        cost_estimate=pl.CostEstimate(
            flops=40 * order**3, bytes_accessed=24 * order * order, transcendentals=0
        ),
    )(lesser, greater, retarded, small)
    return pl.pallas_call(
        functools.partial(finish, tail),
        out_shape=(new, new, new),
        in_specs=[vmem] * 8,
        out_specs=(hbm,) * 3,
        scratch_shapes=[
            whole,
            whole,
            pltpu.SemaphoreType.DMA((1 + 2 * max(order // 256, 1),)),
        ],
        compiler_params=pltpu.CompilerParams(vmem_limit_bytes=16 * 1024 * 1024),
        cost_estimate=pl.CostEstimate(
            flops=8 * order**3, bytes_accessed=12 * order * order, transcendentals=0
        ),
    )(*held)


def solution(mesh):
    split = P("energy", "momentum", None, None, None)
    return jax.shard_map(
        functools.partial(per_device, mesh.shape["energy"], mesh.shape["momentum"]),
        mesh=mesh,
        in_specs=(split, split, split, P(), P(), P()),
        out_specs=(split, split, split),
        check_vma=False,
    )
```

```python
import functools

import jax
import jax.numpy as jnp
import numpy as np
from jax import lax
from jax.experimental import pallas as pl
from jax.experimental.pallas import tpu as pltpu
from jax.sharding import PartitionSpec as P

MESH = pl.DeviceIdType.MESH
STEP = 128
GRAIN = 2.0**27


def dot(a, b):
    return jnp.dot(a, b, preferred_element_type=jnp.float32)


def dot_t(a, b):
    return lax.dot_general(a, b, (((1,), (1,)), ((), ())), preferred_element_type=jnp.float32)


def products(ret, sigma, at, half_less, less_at, width):
    both = jnp.concatenate([sigma[0, :, at], sigma[1, :, at]], axis=1)
    by_re, by_im = dot(ret[0], both), dot(ret[1], both)
    more = by_re[:, :width] - by_im[:, width:], by_re[:, width:] + by_im[:, :width]
    wide = tuple((more[x] - half_less[x, :, less_at]) * 0.5 for x in range(2))
    return tuple(v.astype(jnp.bfloat16) for v in more), tuple(v.astype(jnp.bfloat16) for v in wide)


def adjoint_part(ret, half, at, to):
    re, im = half
    right = jnp.concatenate([ret[0, to, at], ret[1, to, at]], axis=1)
    return (
        dot_t(jnp.concatenate([re, im], axis=1), right),
        dot_t(jnp.concatenate([im, -re], axis=1), right),
    )


def dyson_part(ret, half, at, to):
    re, im = half
    right_re, right_im = ret[0, at, to], ret[1, at, to]
    return (
        dot(jnp.concatenate([re, -im], axis=1), jnp.concatenate([right_re, right_im], axis=0)),
        dot(jnp.concatenate([re, im], axis=1), jnp.concatenate([right_im, right_re], axis=0)),
    )


def kernel(sizes, factor, widths, tail, less_ref, more_ref, ret_ref, small_ref, *refs):
    energies, momenta, modes, parts, rows, cols, row_groups, col_groups = sizes
    stages = len(widths)
    less_new, ret_held, tail_less, tail_more, *refs = refs
    sum_more, sum_ret, refs = refs[:2], refs[2:4], refs[4:]
    small, recv_less, recv_more, mixed, send_less, sig_less, half, half_less, *refs = refs
    send_more, refs = refs[:stages], refs[stages:]
    sig_more, refs = refs[: stages - 1] + [tail_more], refs[stages - 1 :]
    send_sem, recv_sem, own_sem, load_sem, ready_sem = refs
    n = energies * momenta
    me = lax.axis_index("energy") * momenta + lax.axis_index("momentum")
    order = row_groups * rows
    bits = n.bit_length() - 1
    mine = [lax.rem(lax.div(me, 1 << b), 2) for b in range(bits)]

    def partner(d):
        other = 0
        for b in range(bits):
            flip = (d >> b) % 2 if isinstance(d, int) else lax.rem(lax.div(d, 1 << b), 2)
            other += (mine[b] + flip - 2 * mine[b] * flip) * (1 << b)
        return other

    def place(d):
        return lax.div(d, momenta), lax.rem(d, momenta)

    quarter = n // 4
    low = quarter.bit_length() - 1
    my_quarter = lax.div(me, quarter)
    my_half = lax.div(my_quarter, 2)
    far_half = 2 * (1 - my_half)
    near_quarter = 4 * my_half + 1 - my_quarter

    def others(act, ending=False, first=True, which=("low", "high")):
        def target(q, t, fixed):
            if fixed:
                return q * quarter + t
            other = q * quarter
            for b in range(low):
                flip = lax.rem(lax.div(quarter - 1 - t, 1 << b), 2)
                other += (mine[b] + flip - 2 * mine[b] * flip) * (1 << b)
            return other

        def blend(quarters, fixed, skip=0):
            def at(t, carry):
                for q in quarters:
                    act(target(q, t, fixed))
                return carry

            lax.fori_loop(0, quarter - skip, at, 0)

        def own(t, carry):
            act(target(my_quarter, t, False))
            return carry

        skip = 0 if first else 1
        if skip:
            act((far_half + 1 - lax.rem(my_quarter, 2)) * quarter + lax.rem(me, quarter))
        if "low" in which:
            blend([far_half], ending, skip)
            blend([near_quarter], ending)
        if "high" in which:
            blend([far_half + 1], ending, skip)
            lax.fori_loop(0, quarter - 1, own, 0)

    def piece(ref, lead, d, count):
        row = pl.multiple_of(lax.rem(d, row_groups) * rows, rows)
        rest = lax.div(d, row_groups)
        col = pl.multiple_of(lax.rem(rest, col_groups) * count, count)
        part = lax.div(rest, col_groups) * parts
        index = (pl.ds(part, parts), pl.ds(row, rows), pl.ds(col, count))
        return ref.at[(0,) * lead + index]

    def signal(sem, d):
        pl.semaphore_signal(sem, inc=1, device_id=place(d), device_id_type=MESH)

    barrier = pltpu.get_barrier_semaphore()
    for b in range(bits):
        signal(barrier, partner(1 << b))
    loads = [
        pltpu.make_async_copy(piece(less_ref, 2, me, cols), recv_less.at[me], own_sem.at[0]),
        pltpu.make_async_copy(piece(more_ref, 2, me, cols), recv_more.at[me], own_sem.at[1]),
        pltpu.make_async_copy(ret_ref.at[0, 0], ret_held, load_sem.at[0]),
        pltpu.make_async_copy(small_ref, small, load_sem.at[1]),
    ]
    for load in loads:
        load.start()

    def forward(ref, landing, which):
        def send(d):
            pltpu.make_async_remote_copy(
                src_ref=piece(ref, 2, d, cols),
                dst_ref=landing.at[me],
                send_sem=send_sem.at[which],
                recv_sem=recv_sem.at[which],
                device_id=place(d),
                device_id_type=MESH,
            ).start()

        return send

    def back(ref, landing, count, which, ending=False, targets=("low", "high")):
        def send(d):
            pltpu.make_async_remote_copy(
                src_ref=ref.at[d],
                dst_ref=piece(landing, 0, me, count),
                send_sem=send_sem.at[which],
                recv_sem=recv_sem.at[which],
                device_id=place(d),
                device_id_type=MESH,
            ).start()

        others(send, ending, which=targets)

    def wait_all(sem, ref):
        span = ref.at[pl.ds(0, n - 1)]
        pltpu.make_async_copy(span, span, sem).wait()

    send = forward(less_ref, recv_less, 0)
    send_more_forward = forward(more_ref, recv_more, 1)
    for level in range(bits):
        if level == 0:
            pl.semaphore_wait(barrier, bits)
        else:
            pl.semaphore_wait(ready_sem.at[level - 1], bits)
        if level < bits - 1:
            for b in range(bits):
                signal(ready_sem.at[level], partner(1 << b))
        for d in range(n - 1, 0, -1):
            if d.bit_count() == level + 1:
                send(partner(d))
                if d == n // 2:
                    send_more_forward(partner(d))
    others(send_more_forward, first=False)

    mixed[:, energies] = jnp.zeros((modes, momenta, parts, rows, cols), jnp.float32)

    def coupling(m, k, q):
        return small[m, k, q].astype(jnp.float32)

    def mix(recv, send, add_below, add_above, begin, count):
        step = min(count, max(4096 // rows, 128))
        blocks = parts * (count // step)

        def spot(i):
            b = lax.rem(i, blocks)
            col = lax.rem(b, count // step) * step
            return lax.div(i, blocks), lax.div(b, count // step), pl.multiple_of(col, step)

        def over_momenta(i, carry):
            s, part, col = spot(i)
            at = pl.ds(begin + col, step)
            terms = [recv[s * momenta + q, part, :, at].astype(jnp.float32) for q in range(momenta)]
            for m in range(modes):
                for k in range(momenta):
                    total = coupling(m, k, 0) * terms[0]
                    for q in range(1, momenta):
                        total += coupling(m, k, q) * terms[q]
                    mixed[m, s, k, part, :, at] = total
            return carry

        lax.fori_loop(0, energies * blocks, over_momenta, 0)

        def over_energies(i, carry):
            j, part, col = spot(i)
            at, to = pl.ds(begin + col, step), pl.ds(col, step)
            for k in range(momenta):
                total = None
                for m in range(modes):
                    phonons = small[m, momenta + 2, 0].astype(jnp.float32) * (1.0 / GRAIN)
                    for side, add in ((0, add_below), (1, add_above)):
                        slot = small[m, momenta + side, j]
                        term = ((phonons + add) * factor) * mixed[m, slot, k, part, :, at]
                        total = term if total is None else total + term
                send[j * momenta + k, part, :, to] = total.astype(jnp.bfloat16)
            return carry

        lax.fori_loop(0, energies * blocks, over_energies, 0)

    loads[3].wait()
    loads[0].wait()
    wait_all(recv_sem.at[0], recv_less)
    mix(recv_less, send_less, 0.0, 1.0, 0, cols)
    back(send_less, sig_less, cols, 2)
    keep_less = pltpu.make_async_copy(send_less.at[me], piece(sig_less, 0, me, cols), own_sem.at[0])
    keep_less.start()

    loads[1].wait()
    wait_all(recv_sem.at[1], recv_more)
    keeps, begin = [], 0
    for c, width in enumerate(widths):
        mix(recv_more, send_more[c], 1.0, 0.0, begin, width)
        back(send_more[c], sig_more[c], width, 3 + c, c == stages - 1, ("low",))
        keep = pltpu.make_async_copy(send_more[c].at[me], piece(sig_more[c], 0, me, width), own_sem.at[1 + c])
        keep.start()
        keeps.append(keep)
        begin += width
    for c, width in enumerate(widths):
        back(send_more[c], sig_more[c], width, 3 + c, c == stages - 1, ("high",))

    tile = min(order, 256)
    tiles = [pl.ds(t * tile, tile) for t in range(order // tile)]

    loads[2].wait()
    keep_less.wait()
    wait_all(recv_sem.at[2], send_less)
    for at in tiles:
        both_re, both_im = sig_less[0, :, at], sig_less[1, :, at]
        re = dot(ret_held[0], both_re) - dot(ret_held[1], both_im)
        im = dot(ret_held[0], both_im) + dot(ret_held[1], both_re)
        for x, value in enumerate((re, im)):
            half_less[x, :, at] = value
            half[x, :, at] = value.astype(jnp.bfloat16)
    tail_less[...] = half_less[:, :, tail:]
    for to in tiles:
        re, im, right_re, right_im = half[0], half[1], ret_held[0, to, :], ret_held[1, to, :]
        less_new[0, 0, 0, :, to] = (dot_t(re, right_re) + dot_t(im, right_im)).astype(jnp.bfloat16)
        less_new[0, 0, 1, :, to] = (dot_t(im, right_re) - dot_t(re, right_im)).astype(jnp.bfloat16)
    for x in range(2):
        for to in tiles:
            sum_ret[x][:, to] = ret_held[x, :, to].astype(jnp.float32)
            if tail == 0:
                sum_more[x][:, to] = jnp.zeros((order, tile), jnp.float32)

    begin = 0
    for c, width in enumerate(widths):
        keeps[c].wait()
        wait_all(recv_sem.at[3 + c], send_more[c])
        if begin < tail:
            for part in range(width // STEP):
                at = pl.ds(begin + part * STEP, STEP)
                more, wide = products(ret_held, sig_more[c], pl.ds(part * STEP, STEP), half_less, at, STEP)
                for to in tiles:
                    add_more, add_ret = adjoint_part(ret_held, more, at, to), dyson_part(ret_held, wide, at, to)
                    for x in range(2):
                        sum_ret[x][:, to] += add_ret[x]
                        if begin + part == 0:
                            sum_more[x][:, to] = add_more[x]
                        else:
                            sum_more[x][:, to] += add_more[x]
        begin += width
    for which, ref in enumerate([recv_less, recv_more, send_less, *send_more]):
        wait_all(send_sem.at[which], ref)


def finish(tail, less_new, ret_held, tail_less, tail_more, *refs):
    sum_more, sum_ret, refs = refs[:2], refs[2:4], refs[4:]
    less_out, more_out, ret_out, more_new, ret_new, sem = refs
    order = less_new.shape[-1]
    copies = [pltpu.make_async_copy(less_new, less_out, sem.at[0])]
    copies[0].start()
    tile = min(order, 256)
    steps = range(tail, order, STEP)
    halves = []
    for b in steps:
        at = pl.ds(b - tail, STEP)
        halves.append(products(ret_held, tail_more, at, tail_less, at, STEP))
    for t in range(order // tile):
        to = pl.ds(t * tile, tile)
        more, ret = [sum_more[x][:, to] for x in range(2)], [sum_ret[x][:, to] for x in range(2)]
        for b, (half_more, half_ret) in zip(steps, halves):
            add_more = adjoint_part(ret_held, half_more, pl.ds(b, STEP), to)
            add_ret = dyson_part(ret_held, half_ret, pl.ds(b, STEP), to)
            more = [more[x] + add_more[x] for x in range(2)]
            ret = [ret[x] + add_ret[x] for x in range(2)]
        for x in range(2):
            more_new[x, :, to] = more[x].astype(jnp.bfloat16)
            ret_new[x, :, to] = ret[x].astype(jnp.bfloat16)
        for i, (made, out) in enumerate(((more_new, more_out), (ret_new, ret_out))):
            copy = pltpu.make_async_copy(made.at[:, :, to], out.at[0, 0, :, :, to], sem.at[1 + 2 * t + i])
            copy.start()
            copies.append(copy)
    for copy in copies:
        copy.wait()


def per_device(energies, momenta, lesser, greater, retarded, occupation, shift_slots, coupling):
    n = energies * momenta
    modes = coupling.shape[0]
    order = lesser.shape[-1]
    factor = 1.0 / (order * 4.0 * (modes * momenta) ** 0.5)
    row_groups = min(n // 2, order // 16)
    col_groups = n // 2 // row_groups
    parts, rows, cols = 1, order // row_groups, order // col_groups
    sizes = (energies, momenta, modes, parts, rows, cols, row_groups, col_groups)
    vmem = pl.BlockSpec(memory_space=pltpu.VMEM)
    hbm = pl.BlockSpec(memory_space=pltpu.HBM)
    widths = (128, 128, 128, 128) if cols == 512 else (cols,)
    tail = order - widths[-1] if col_groups == 1 else 0
    stages = len(widths)

    def exchanged(width):
        return pltpu.VMEM((n, parts, rows, width), jnp.bfloat16)

    whole = pltpu.VMEM((2, order, order), jnp.bfloat16)
    new = jax.ShapeDtypeStruct(lesser.shape, jnp.bfloat16)
    total = jax.ShapeDtypeStruct((order, order), jnp.float32)
    length = max(energies, momenta, modes)
    packed = (modes, momenta + 3, length)
    last = np.zeros(packed, np.float32)
    last[:, momenta + 2] = GRAIN
    phonons = lax.broadcast_in_dim(occupation, packed, (0,)) * last
    weights = lax.pad(coupling, 0, ((0, 0, 0), (0, 3, 0), (0, length - momenta, 0)))
    slots = lax.pad(shift_slots, 0, ((0, 0, 0), (momenta, 1, 0), (0, length - energies, 0)))
    small = weights + slots + phonons.astype(jnp.int32)
    held = pl.pallas_call(
        functools.partial(kernel, sizes, factor, widths, tail),
        out_shape=(
            new,
            jax.ShapeDtypeStruct((2, order, order), jnp.bfloat16),
            jax.ShapeDtypeStruct((2, order, order - tail), jnp.float32),
            jax.ShapeDtypeStruct((2, order, order - tail), jnp.bfloat16),
            *[total] * 4,
        ),
        in_specs=[hbm] * 4,
        out_specs=(vmem,) * 8,
        scratch_shapes=[
            pltpu.SMEM(small.shape, jnp.int32),
            exchanged(cols),
            exchanged(cols),
            pltpu.VMEM((modes, energies + 1, momenta, parts, rows, cols), jnp.float32),
            exchanged(cols),
            whole,
            whole,
            pltpu.VMEM((2, order, order), jnp.float32),
            *[exchanged(width) for width in widths],
            *[pltpu.VMEM((2, order, width * col_groups), jnp.bfloat16) for width in widths[:-1]],
            pltpu.SemaphoreType.DMA((3 + stages,)),
            pltpu.SemaphoreType.DMA((3 + stages,)),
            pltpu.SemaphoreType.DMA((1 + stages,)),
            pltpu.SemaphoreType.DMA((2,)),
            pltpu.SemaphoreType.REGULAR((n.bit_length() - 2,)),
        ],
        compiler_params=pltpu.CompilerParams(
            collective_id=0, has_side_effects=True, vmem_limit_bytes=47 * 1024 * 1024
        ),
        cost_estimate=pl.CostEstimate(
            flops=40 * order**3, bytes_accessed=24 * order * order, transcendentals=0
        ),
    )(lesser, greater, retarded, small)
    return pl.pallas_call(
        functools.partial(finish, tail),
        out_shape=(new, new, new),
        in_specs=[vmem] * 8,
        out_specs=(hbm,) * 3,
        scratch_shapes=[
            whole,
            whole,
            pltpu.SemaphoreType.DMA((1 + 2 * max(order // 256, 1),)),
        ],
        compiler_params=pltpu.CompilerParams(vmem_limit_bytes=16 * 1024 * 1024),
        cost_estimate=pl.CostEstimate(
            flops=8 * order**3, bytes_accessed=12 * order * order, transcendentals=0
        ),
    )(*held)


def solution(mesh):
    split = P("energy", "momentum", None, None, None)
    return jax.shard_map(
        functools.partial(per_device, mesh.shape["energy"], mesh.shape["momentum"]),
        mesh=mesh,
        in_specs=(split, split, split, P(), P(), P()),
        out_specs=(split, split, split),
        check_vma=False,
    )
```

```python
import functools

import jax
import jax.numpy as jnp
import numpy as np
from jax import lax
from jax.experimental import pallas as pl
from jax.experimental.pallas import tpu as pltpu
from jax.sharding import PartitionSpec as P

MESH = pl.DeviceIdType.MESH
STEP = 128
GRAIN = 2.0**27


def dot(a, b):
    return jnp.dot(a, b, preferred_element_type=jnp.float32)


def dot_t(a, b):
    return lax.dot_general(a, b, (((1,), (1,)), ((), ())), preferred_element_type=jnp.float32)


def products(ret, sigma, at, half_less, less_at, width):
    both = jnp.concatenate([sigma[0, :, at], sigma[1, :, at]], axis=1)
    by_re, by_im = dot(ret[0], both), dot(ret[1], both)
    more = by_re[:, :width] - by_im[:, width:], by_re[:, width:] + by_im[:, :width]
    wide = tuple((more[x] - half_less[x, :, less_at]) * 0.5 for x in range(2))
    return tuple(v.astype(jnp.bfloat16) for v in more), tuple(v.astype(jnp.bfloat16) for v in wide)


def adjoint_part(ret, half, at, to):
    re, im = half
    right = jnp.concatenate([ret[0, to, at], ret[1, to, at]], axis=1)
    return (
        dot_t(jnp.concatenate([re, im], axis=1), right),
        dot_t(jnp.concatenate([im, -re], axis=1), right),
    )


def dyson_part(ret, half, at, to):
    re, im = half
    right_re, right_im = ret[0, at, to], ret[1, at, to]
    return (
        dot(jnp.concatenate([re, -im], axis=1), jnp.concatenate([right_re, right_im], axis=0)),
        dot(jnp.concatenate([re, im], axis=1), jnp.concatenate([right_im, right_re], axis=0)),
    )


def kernel(sizes, factor, widths, tail, less_ref, more_ref, ret_ref, small_ref, *refs):
    energies, momenta, modes, parts, rows, cols, row_groups, col_groups = sizes
    stages = len(widths)
    less_new, ret_held, tail_less, tail_more, *refs = refs
    sum_more, sum_ret, refs = refs[:2], refs[2:4], refs[4:]
    small, recv_less, recv_more, mixed, send_less, sig_less, half, half_less, *refs = refs
    send_more, refs = refs[:stages], refs[stages:]
    sig_more, refs = refs[: stages - 1] + [tail_more], refs[stages - 1 :]
    send_sem, recv_sem, own_sem, load_sem, ready_sem = refs
    n = energies * momenta
    me = lax.axis_index("energy") * momenta + lax.axis_index("momentum")
    order = row_groups * rows
    bits = n.bit_length() - 1
    mine = [lax.rem(lax.div(me, 1 << b), 2) for b in range(bits)]

    def partner(d):
        other = 0
        for b in range(bits):
            flip = (d >> b) % 2 if isinstance(d, int) else lax.rem(lax.div(d, 1 << b), 2)
            other += (mine[b] + flip - 2 * mine[b] * flip) * (1 << b)
        return other

    def place(d):
        return lax.div(d, momenta), lax.rem(d, momenta)

    quarter = n // 4
    low = quarter.bit_length() - 1
    my_quarter = lax.div(me, quarter)
    my_half = lax.div(my_quarter, 2)
    far_half = 2 * (1 - my_half)
    near_quarter = 4 * my_half + 1 - my_quarter

    def others(act, ending=False, first=True, which=("low", "high")):
        def target(q, t, fixed):
            if fixed:
                return q * quarter + t
            other = q * quarter
            for b in range(low):
                flip = lax.rem(lax.div(quarter - 1 - t, 1 << b), 2)
                other += (mine[b] + flip - 2 * mine[b] * flip) * (1 << b)
            return other

        def blend(quarters, fixed, skip=0):
            def at(t, carry):
                for q in quarters:
                    act(target(q, t, fixed))
                return carry

            lax.fori_loop(0, quarter - skip, at, 0)

        def own(t, carry):
            act(target(my_quarter, t, False))
            return carry

        skip = 0 if first else 1
        if skip:
            act((far_half + 1 - lax.rem(my_quarter, 2)) * quarter + lax.rem(me, quarter))
        if len(which) == 2:
            blend([far_half, far_half + 1], ending, skip)
            blend([near_quarter], ending)
            lax.fori_loop(0, quarter - 1, own, 0)
        elif "low" in which:
            blend([far_half], ending, skip)
            blend([near_quarter], ending)
        else:
            blend([far_half + 1], ending, skip)
            lax.fori_loop(0, quarter - 1, own, 0)

    def piece(ref, lead, d, count):
        row = pl.multiple_of(lax.rem(d, row_groups) * rows, rows)
        rest = lax.div(d, row_groups)
        col = pl.multiple_of(lax.rem(rest, col_groups) * count, count)
        part = lax.div(rest, col_groups) * parts
        index = (pl.ds(part, parts), pl.ds(row, rows), pl.ds(col, count))
        return ref.at[(0,) * lead + index]

    def signal(sem, d):
        pl.semaphore_signal(sem, inc=1, device_id=place(d), device_id_type=MESH)

    barrier = pltpu.get_barrier_semaphore()
    for b in range(bits):
        signal(barrier, partner(1 << b))
    loads = [
        pltpu.make_async_copy(piece(less_ref, 2, me, cols), recv_less.at[me], own_sem.at[0]),
        pltpu.make_async_copy(piece(more_ref, 2, me, cols), recv_more.at[me], own_sem.at[1]),
        pltpu.make_async_copy(ret_ref.at[0, 0], ret_held, load_sem.at[0]),
        pltpu.make_async_copy(small_ref, small, load_sem.at[1]),
    ]
    for load in loads:
        load.start()

    def forward(ref, landing, which):
        def send(d):
            pltpu.make_async_remote_copy(
                src_ref=piece(ref, 2, d, cols),
                dst_ref=landing.at[me],
                send_sem=send_sem.at[which],
                recv_sem=recv_sem.at[which],
                device_id=place(d),
                device_id_type=MESH,
            ).start()

        return send

    def back(ref, landing, count, which, ending=False, targets=("low", "high")):
        def send(d):
            pltpu.make_async_remote_copy(
                src_ref=ref.at[d],
                dst_ref=piece(landing, 0, me, count),
                send_sem=send_sem.at[which],
                recv_sem=recv_sem.at[which],
                device_id=place(d),
                device_id_type=MESH,
            ).start()

        others(send, ending, which=targets)

    def wait_all(sem, ref):
        span = ref.at[pl.ds(0, n - 1)]
        pltpu.make_async_copy(span, span, sem).wait()

    send = forward(less_ref, recv_less, 0)
    send_more_forward = forward(more_ref, recv_more, 1)
    for level in range(bits):
        if level == 0:
            pl.semaphore_wait(barrier, bits)
        else:
            pl.semaphore_wait(ready_sem.at[level - 1], bits)
        if level < bits - 1:
            for b in range(bits):
                signal(ready_sem.at[level], partner(1 << b))
        for d in range(n - 1, 0, -1):
            if d.bit_count() == level + 1:
                send(partner(d))
                if d == n // 2:
                    send_more_forward(partner(d))
    others(send_more_forward, first=False)

    mixed[:, energies] = jnp.zeros((modes, momenta, parts, rows, cols), jnp.float32)

    def coupling(m, k, q):
        return small[m, k, q].astype(jnp.float32)

    def mix(recv, send, add_below, add_above, begin, count):
        step = min(count, max(4096 // rows, 128))
        blocks = parts * (count // step)

        def spot(i):
            b = lax.rem(i, blocks)
            col = lax.rem(b, count // step) * step
            return lax.div(i, blocks), lax.div(b, count // step), pl.multiple_of(col, step)

        def over_momenta(i, carry):
            s, part, col = spot(i)
            at = pl.ds(begin + col, step)
            terms = [recv[s * momenta + q, part, :, at].astype(jnp.float32) for q in range(momenta)]
            for m in range(modes):
                for k in range(momenta):
                    total = coupling(m, k, 0) * terms[0]
                    for q in range(1, momenta):
                        total += coupling(m, k, q) * terms[q]
                    mixed[m, s, k, part, :, at] = total
            return carry

        lax.fori_loop(0, energies * blocks, over_momenta, 0)

        def over_energies(i, carry):
            j, part, col = spot(i)
            at, to = pl.ds(begin + col, step), pl.ds(col, step)
            for k in range(momenta):
                total = None
                for m in range(modes):
                    phonons = small[m, momenta + 2, 0].astype(jnp.float32) * (1.0 / GRAIN)
                    for side, add in ((0, add_below), (1, add_above)):
                        slot = small[m, momenta + side, j]
                        term = ((phonons + add) * factor) * mixed[m, slot, k, part, :, at]
                        total = term if total is None else total + term
                send[j * momenta + k, part, :, to] = total.astype(jnp.bfloat16)
            return carry

        lax.fori_loop(0, energies * blocks, over_energies, 0)

    loads[3].wait()
    loads[0].wait()
    wait_all(recv_sem.at[0], recv_less)
    mix(recv_less, send_less, 0.0, 1.0, 0, cols)
    back(send_less, sig_less, cols, 2)
    keep_less = pltpu.make_async_copy(send_less.at[me], piece(sig_less, 0, me, cols), own_sem.at[0])
    keep_less.start()

    loads[1].wait()
    wait_all(recv_sem.at[1], recv_more)
    keeps, begin = [], 0
    for c, width in enumerate(widths):
        mix(recv_more, send_more[c], 1.0, 0.0, begin, width)
        back(send_more[c], sig_more[c], width, 3 + c, c == stages - 1, ("low",))
        keep = pltpu.make_async_copy(send_more[c].at[me], piece(sig_more[c], 0, me, width), own_sem.at[1 + c])
        keep.start()
        keeps.append(keep)
        begin += width
    for c, width in enumerate(widths):
        back(send_more[c], sig_more[c], width, 3 + c, c == stages - 1, ("high",))

    tile = min(order, 256)
    tiles = [pl.ds(t * tile, tile) for t in range(order // tile)]

    loads[2].wait()
    keep_less.wait()
    wait_all(recv_sem.at[2], send_less)
    for at in tiles:
        both_re, both_im = sig_less[0, :, at], sig_less[1, :, at]
        re = dot(ret_held[0], both_re) - dot(ret_held[1], both_im)
        im = dot(ret_held[0], both_im) + dot(ret_held[1], both_re)
        for x, value in enumerate((re, im)):
            half_less[x, :, at] = value
            half[x, :, at] = value.astype(jnp.bfloat16)
    tail_less[...] = half_less[:, :, tail:]
    for to in tiles:
        re, im, right_re, right_im = half[0], half[1], ret_held[0, to, :], ret_held[1, to, :]
        less_new[0, 0, 0, :, to] = (dot_t(re, right_re) + dot_t(im, right_im)).astype(jnp.bfloat16)
        less_new[0, 0, 1, :, to] = (dot_t(im, right_re) - dot_t(re, right_im)).astype(jnp.bfloat16)
    for x in range(2):
        for to in tiles:
            sum_ret[x][:, to] = ret_held[x, :, to].astype(jnp.float32)
            if tail == 0:
                sum_more[x][:, to] = jnp.zeros((order, tile), jnp.float32)

    begin = 0
    for c, width in enumerate(widths):
        keeps[c].wait()
        wait_all(recv_sem.at[3 + c], send_more[c])
        if begin < tail:
            for part in range(width // STEP):
                at = pl.ds(begin + part * STEP, STEP)
                more, wide = products(ret_held, sig_more[c], pl.ds(part * STEP, STEP), half_less, at, STEP)
                for to in tiles:
                    add_more, add_ret = adjoint_part(ret_held, more, at, to), dyson_part(ret_held, wide, at, to)
                    for x in range(2):
                        sum_ret[x][:, to] += add_ret[x]
                        if begin + part == 0:
                            sum_more[x][:, to] = add_more[x]
                        else:
                            sum_more[x][:, to] += add_more[x]
        begin += width
    for which, ref in enumerate([recv_less, recv_more, send_less, *send_more]):
        wait_all(send_sem.at[which], ref)


def finish(tail, less_new, ret_held, tail_less, tail_more, *refs):
    sum_more, sum_ret, refs = refs[:2], refs[2:4], refs[4:]
    less_out, more_out, ret_out, more_new, ret_new, sem = refs
    order = less_new.shape[-1]
    copies = [pltpu.make_async_copy(less_new, less_out, sem.at[0])]
    copies[0].start()
    tile = min(order, 256)
    steps = range(tail, order, STEP)
    halves = []
    for b in steps:
        at = pl.ds(b - tail, STEP)
        halves.append(products(ret_held, tail_more, at, tail_less, at, STEP))
    for t in range(order // tile):
        to = pl.ds(t * tile, tile)
        more, ret = [sum_more[x][:, to] for x in range(2)], [sum_ret[x][:, to] for x in range(2)]
        for b, (half_more, half_ret) in zip(steps, halves):
            add_more = adjoint_part(ret_held, half_more, pl.ds(b, STEP), to)
            add_ret = dyson_part(ret_held, half_ret, pl.ds(b, STEP), to)
            more = [more[x] + add_more[x] for x in range(2)]
            ret = [ret[x] + add_ret[x] for x in range(2)]
        for x in range(2):
            more_new[x, :, to] = more[x].astype(jnp.bfloat16)
            ret_new[x, :, to] = ret[x].astype(jnp.bfloat16)
        for i, (made, out) in enumerate(((more_new, more_out), (ret_new, ret_out))):
            copy = pltpu.make_async_copy(made.at[:, :, to], out.at[0, 0, :, :, to], sem.at[1 + 2 * t + i])
            copy.start()
            copies.append(copy)
    for copy in copies:
        copy.wait()


def per_device(energies, momenta, lesser, greater, retarded, occupation, shift_slots, coupling):
    n = energies * momenta
    modes = coupling.shape[0]
    order = lesser.shape[-1]
    factor = 1.0 / (order * 4.0 * (modes * momenta) ** 0.5)
    row_groups = min(n // 2, order // 16)
    col_groups = n // 2 // row_groups
    parts, rows, cols = 1, order // row_groups, order // col_groups
    sizes = (energies, momenta, modes, parts, rows, cols, row_groups, col_groups)
    vmem = pl.BlockSpec(memory_space=pltpu.VMEM)
    hbm = pl.BlockSpec(memory_space=pltpu.HBM)
    widths = (128, 128, 128, 128) if cols == 512 else (cols,)
    tail = order - widths[-1] if col_groups == 1 else 0
    stages = len(widths)

    def exchanged(width):
        return pltpu.VMEM((n, parts, rows, width), jnp.bfloat16)

    whole = pltpu.VMEM((2, order, order), jnp.bfloat16)
    new = jax.ShapeDtypeStruct(lesser.shape, jnp.bfloat16)
    total = jax.ShapeDtypeStruct((order, order), jnp.float32)
    length = max(energies, momenta, modes)
    packed = (modes, momenta + 3, length)
    last = np.zeros(packed, np.float32)
    last[:, momenta + 2] = GRAIN
    phonons = lax.broadcast_in_dim(occupation, packed, (0,)) * last
    weights = lax.pad(coupling, 0, ((0, 0, 0), (0, 3, 0), (0, length - momenta, 0)))
    slots = lax.pad(shift_slots, 0, ((0, 0, 0), (momenta, 1, 0), (0, length - energies, 0)))
    small = weights + slots + phonons.astype(jnp.int32)
    held = pl.pallas_call(
        functools.partial(kernel, sizes, factor, widths, tail),
        out_shape=(
            new,
            jax.ShapeDtypeStruct((2, order, order), jnp.bfloat16),
            jax.ShapeDtypeStruct((2, order, order - tail), jnp.float32),
            jax.ShapeDtypeStruct((2, order, order - tail), jnp.bfloat16),
            *[total] * 4,
        ),
        in_specs=[hbm] * 4,
        out_specs=(vmem,) * 8,
        scratch_shapes=[
            pltpu.SMEM(small.shape, jnp.int32),
            exchanged(cols),
            exchanged(cols),
            pltpu.VMEM((modes, energies + 1, momenta, parts, rows, cols), jnp.float32),
            exchanged(cols),
            whole,
            whole,
            pltpu.VMEM((2, order, order), jnp.float32),
            *[exchanged(width) for width in widths],
            *[pltpu.VMEM((2, order, width * col_groups), jnp.bfloat16) for width in widths[:-1]],
            pltpu.SemaphoreType.DMA((3 + stages,)),
            pltpu.SemaphoreType.DMA((3 + stages,)),
            pltpu.SemaphoreType.DMA((1 + stages,)),
            pltpu.SemaphoreType.DMA((2,)),
            pltpu.SemaphoreType.REGULAR((n.bit_length() - 2,)),
        ],
        compiler_params=pltpu.CompilerParams(
            collective_id=0, has_side_effects=True, vmem_limit_bytes=47 * 1024 * 1024
        ),
        cost_estimate=pl.CostEstimate(
            flops=40 * order**3, bytes_accessed=24 * order * order, transcendentals=0
        ),
    )(lesser, greater, retarded, small)
    return pl.pallas_call(
        functools.partial(finish, tail),
        out_shape=(new, new, new),
        in_specs=[vmem] * 8,
        out_specs=(hbm,) * 3,
        scratch_shapes=[
            whole,
            whole,
            pltpu.SemaphoreType.DMA((1 + 2 * max(order // 256, 1),)),
        ],
        compiler_params=pltpu.CompilerParams(vmem_limit_bytes=16 * 1024 * 1024),
        cost_estimate=pl.CostEstimate(
            flops=8 * order**3, bytes_accessed=12 * order * order, transcendentals=0
        ),
    )(*held)


def solution(mesh):
    split = P("energy", "momentum", None, None, None)
    return jax.shard_map(
        functools.partial(per_device, mesh.shape["energy"], mesh.shape["momentum"]),
        mesh=mesh,
        in_specs=(split, split, split, P(), P(), P()),
        out_specs=(split, split, split),
        check_vma=False,
    )
```
